32 devices in a mesh: member: 8 (over z, core), fsdp: 4 (over y, x).
Axes of the slice: x: 2, y: 2, z: 4, core: 2. Of those that a mesh axis runs over, the one named last changes fastest.
Arguments:
- attn_queries: bfloat16 [8, 512, 16, 128], P('member', 'fsdp'), may hold values from -27 to 27
- attn_keys: bfloat16 [8, 512, 16, 128], P('member', 'fsdp'), may hold values from -7.5 to 7.5
- attn_values: bfloat16 [8, 512, 16, 128], P('member', 'fsdp'), may hold values from -6 to 6
- out_grad: bfloat16 [8, 512, 4096], P('member', 'fsdp'), may hold values from -6 to 6
- out_proj: bfloat16 [8, 4096, 2048], P('member', 'fsdp'), may hold values from -0.125 to 0.125
- first_moment: float32 [8, 4096, 2048], P('member', 'fsdp'), may hold values from -4 to 4
- second_moment: float32 [8, 4096, 2048], P('member', 'fsdp'), may hold values from 0.05 to 5
- explore_noise: bfloat16 [8, 4096, 2048], P('member', 'fsdp'), may hold values from -0.4375 to 0.4375
- donor_index: int32 [8], replicated, may hold values from 0 to 7, as said below
- copy_flag: int32 [8], replicated, may hold values from 0 to 1, as said below
Outputs:
- new_proj: bfloat16 [8, 4096, 2048], P('member', 'fsdp')
- new_first: float32 [8, 4096, 2048], P('member', 'fsdp')
- new_second: float32 [8, 4096, 2048], P('member', 'fsdp')
The draws below stay inside these ranges and needn't reach their ends.
Inputs may be any that keep to these rules, and one draw needn't show every extreme that they name: `donor_index`: every entry names one of the same four members (which four may differ from call to call); none of those four has copy_flag 1. `copy_flag`: exactly 2 entries are 1.
All inputs are finite; a program needn't handle non-finite values.
Results may differ from the reference program's by a relative error of at most 0.017.
Values may be sent and summed in bfloat16 or wider, within the bound.
A program may use at most 128 MiB of HBM per device.

```python
import math
import jax
import jax.numpy as jnp
from jax import lax

D = 4096
HEAD_DIM = 128
HEADS = 16
TOK_DEV = 128
SEQ = 512
HID = 2048
MEMBERS = 8
N_FSDP = 4


def drawn_pair(key):
    base = jax.random.fold_in(key, 29)
    key_query, key_key = jax.random.split(base, 2)
    shape = (MEMBERS, SEQ, HEADS, HEAD_DIM)
    queries = jnp.clip(jax.random.normal(key_query, shape, jnp.float32), -4.0, 4.0)
    keys = jnp.clip(jax.random.normal(key_key, shape, jnp.float32), -4.0, 4.0)
    return (queries, keys)


def draw_attn_queries(key, part):
    return drawn_pair(key)[0].astype(jnp.bfloat16)


def draw_attn_keys(key, part):
    return drawn_pair(key)[1].astype(jnp.bfloat16)


def pairing(key):
    base = jax.random.fold_in(key, 41)
    key_order, key_pick = jax.random.split(base, 2)
    middle = (jax.random.permutation(key_order, MEMBERS - 2) + 1).astype(jnp.int32)
    ends = jnp.array([0, MEMBERS - 1], jnp.int32)
    order = jnp.concatenate([ends, middle]).astype(jnp.int32)
    quarter = MEMBERS // 4
    picked = jax.random.randint(key_pick, (MEMBERS,), 0, quarter).astype(jnp.int32)
    picked = picked.at[order[MEMBERS - 1]].set(0).at[order[MEMBERS - 2]].set(1)
    donors = order[picked]
    flags = jnp.zeros((MEMBERS,), jnp.int32).at[order[MEMBERS - quarter:]].set(1)
    return (donors, flags)


def draw_donor_index(key, part):
    return pairing(key)[0]


def draw_copy_flag(key, part):
    return pairing(key)[1]


def with_spikes(result, rng, source, target, blocks, factor):
    owner, partner = [(jnp.arange(result.shape[dim]) // (result.shape[dim] // blocks)).reshape([-1 if axis == dim else 1 for axis in range(result.ndim)]) for dim in (source, target)]
    chosen = jax.random.permutation(rng, blocks)[partner]
    strong = (owner == chosen) | (owner == (partner + blocks // 2) % blocks)
    return jnp.where(strong, factor * result, result)


def block_scale(rng, extent, pieces, low, top_value):
    level, own = 1.0, jax.random.fold_in(rng, 6)
    for dim, shards_of in pieces:
        draws = jnp.exp(jax.random.uniform(jax.random.fold_in(own, dim), (shards_of,), jnp.float32, low / len(pieces), top_value / len(pieces)))
        level = level * jnp.repeat(draws, extent[dim] // shards_of).reshape([-1 if axis == dim else 1 for axis in range(len(extent))])
    return level


def bell_draw(own_key, extent, spread, bound, pieces=(), kind=jnp.bfloat16):
    loudness = block_scale(own_key, extent, pieces, -0.22, 0.18) if pieces else 1.0
    entries = jax.random.normal(own_key, extent, jnp.float32) * spread * loudness
    return jnp.minimum(jnp.maximum(entries, -bound), bound).astype(kind)


def gaussian_with(own_key, shape, scale, reach, cuts, heavy, held_as=jnp.bfloat16):
    values = scale * jax.random.normal(own_key, shape, jnp.float32)
    if cuts:
        values = values * block_scale(own_key, shape, cuts, -0.22, 0.18)
    return jnp.clip(with_spikes(values, jax.random.fold_in(own_key, 3), *heavy), -reach, reach).astype(held_as)


def setup_inputs(seed: int = 0) -> dict:
    splits = jax.random.split(jax.random.key(seed), 11)
    attn_queries = draw_attn_queries(jax.random.fold_in(splits[10], 71), 0)
    attn_keys = draw_attn_keys(jax.random.fold_in(splits[10], 71), 0)
    attn_values = bell_draw(splits[2], (MEMBERS, SEQ, HEADS, HEAD_DIM), 1.0, 6.0, ((0, 8), (1, 4)))
    out_grad = gaussian_with(splits[3], (MEMBERS, SEQ, D), 1.0, 6.0, ((0, 8), (1, 4)), (1, 2, 4, 2.0))
    out_proj = bell_draw(splits[4], (MEMBERS, D, HID), HID ** -0.5, 0.125, ((0, 8), (1, 4)))
    first_moment = bell_draw(splits[5], (MEMBERS, D, HID), 0.5, 4.0, ((0, 8), (1, 4)), jnp.float32)
    second_moment = jnp.clip(jnp.exp(math.log(5.0) - 4.6051702 * jax.random.uniform(splits[6], (MEMBERS, D, HID), jnp.float32) ** block_scale(splits[6], (MEMBERS, D, HID), ((0, 8), (1, 4)), -0.2, 0.2)), 0.05, 5.0)
    explore_noise = bell_draw(splits[7], (MEMBERS, D, HID), 0.03, 0.4375, ((0, 8), (1, 4)))
    donor_index = draw_donor_index(jax.random.fold_in(splits[10], 71), 0)
    copy_flag = draw_copy_flag(jax.random.fold_in(splits[10], 71), 0)
    return dict(attn_queries=attn_queries, attn_keys=attn_keys, attn_values=attn_values, out_grad=out_grad, out_proj=out_proj, first_moment=first_moment, second_moment=second_moment, explore_noise=explore_noise, donor_index=donor_index, copy_flag=copy_flag)


masked_value = -1e+30
beta_first = 0.9
beta_second = 0.95
learn_rate = 0.001
decay_rate = 0.1
epsilon = 1e-08

def member_context(queries, keys, values):
    sequence = queries.shape[0]
    scores = jnp.einsum('qhe,khe->hqk', queries.astype(jnp.float32), keys.astype(jnp.float32)) * HEAD_DIM ** (-0.5)
    position = jnp.arange(sequence, dtype=jnp.int32)
    allowed = position[:, None] >= position[None, :]
    scores = jnp.where(allowed[None], scores, masked_value)
    maximum = lax.optimization_barrier(jnp.max(scores, axis=-1, keepdims=True))
    weights = jnp.where(allowed[None], jnp.exp(scores - maximum), jnp.float32(0.0))
    totals = lax.optimization_barrier(jnp.sum(weights, axis=-1))
    rounded = weights.astype(jnp.bfloat16)
    context = jnp.einsum('hqk,khe->qhe', rounded.astype(jnp.float32), values.astype(jnp.float32))
    context = context / jnp.transpose(totals)[:, :, None]
    return context.astype(jnp.bfloat16).reshape(sequence, HEADS * HEAD_DIM)

def member_step(items):
    queries, keys, values, grad_out, weight, first, second = items
    context = member_context(queries, keys, values)
    blocks = (context.reshape(N_FSDP, TOK_DEV, HEADS * HEAD_DIM), grad_out.reshape(N_FSDP, TOK_DEV, D))

    def add_block(running, pair):
        context_rows, grad_rows = pair
        partial_sum = jnp.dot(grad_rows.T, context_rows, preferred_element_type=jnp.float32)
        partial_sum = lax.optimization_barrier(partial_sum.astype(jnp.bfloat16)).astype(jnp.float32)
        return (running + partial_sum, None)
    gradient, unused = lax.scan(add_block, jnp.zeros((D, HEADS * HEAD_DIM), jnp.float32), blocks)
    moment_one = beta_first * first + (1.0 - beta_first) * gradient
    moment_two = beta_second * second + (1.0 - beta_second) * gradient * gradient
    bias_first = 1.0 - beta_first ** 100.0
    bias_second = 1.0 - beta_second ** 100.0
    step_size = moment_one / bias_first / (jnp.sqrt(moment_two / bias_second) + epsilon)
    weight_float = weight.astype(jnp.float32)
    updated = (weight_float - learn_rate * (step_size + decay_rate * weight_float)).astype(jnp.bfloat16)
    return (updated, moment_one, moment_two)

def reference(attn_queries, attn_keys, attn_values, out_grad, out_proj, first_moment, second_moment, explore_noise, donor_index, copy_flag):
    updated, moment_one, moment_two = lax.map(member_step, (attn_queries, attn_keys, attn_values, out_grad, out_proj, first_moment, second_moment))
    source = jnp.where(copy_flag == 1, donor_index, jnp.arange(MEMBERS, dtype=jnp.int32)).astype(jnp.int32)
    chosen = jnp.take(updated, source, axis=0)
    new_first = jnp.take(moment_one, source, axis=0)
    new_second = jnp.take(moment_two, source, axis=0)
    flagged = (copy_flag == 1)[:, None, None]
    perturbed = (chosen.astype(jnp.float32) + explore_noise.astype(jnp.float32)).astype(jnp.bfloat16)
    new_proj = jnp.where(flagged, perturbed, chosen)
    return (new_proj, new_first, new_second)
```

```python
import functools

import jax
import jax.numpy as jnp
from jax import lax
from jax.experimental import pallas as pl
from jax.experimental.pallas import tpu as pltpu
from jax.sharding import PartitionSpec as P

masked_value = -1e30
beta_first = 0.9
beta_second = 0.95
learn_rate = 0.001
decay_rate = 0.1
epsilon = 1e-08
chunk_rows = 32
lag = 2
MESH = pl.DeviceIdType.MESH


def chain_kernel(size, chunks, flags, own_hbm, out_hbm, own, up, down, up_send, up_recv, down_send, down_recv, local_sem):
    me = lax.axis_index("member")
    last = size - 1
    load = pltpu.make_async_copy(own_hbm, own, local_sem)
    load.start()
    barrier = pltpu.get_barrier_semaphore()

    @pl.when(me > 0)
    def _():
        pl.semaphore_signal(barrier, inc=1, device_id={"member": me - 1}, device_id_type=MESH)

    @pl.when(me < last)
    def _():
        pl.semaphore_signal(barrier, inc=1, device_id={"member": me + 1}, device_id_type=MESH)

    @pl.when(jnp.logical_or(me == 0, me == last))
    def _():
        pl.semaphore_wait(barrier, 1)

    @pl.when(jnp.logical_and(me > 0, me < last))
    def _():
        pl.semaphore_wait(barrier, 2)

    load.wait()

    def rows(chunk):
        return pl.ds(pl.multiple_of(chunk * chunk_rows, chunk_rows), chunk_rows)

    def copy(buffer, send, recv, chunk, target):
        return pltpu.make_async_remote_copy(
            src_ref=buffer.at[rows(chunk)],
            dst_ref=buffer.at[rows(chunk)],
            send_sem=send.at[chunk],
            recv_sem=recv.at[chunk],
            device_id={"member": target},
            device_id_type=MESH,
        )

    def advance(chunk, buffer, send, recv, first, final, target, flag):
        @pl.when(jnp.logical_and(chunk >= 0, chunk < chunks))
        def _():
            @pl.when(first)
            def _():
                buffer[rows(chunk), :] = own[rows(chunk), :]

            @pl.when(jnp.logical_not(first))
            def _():
                copy(buffer, send, recv, chunk, target).wait_recv()
                buffer[rows(chunk), :] = lax.select(flag == 1, own[rows(chunk), :], buffer[rows(chunk), :])

            @pl.when(jnp.logical_not(final))
            def _():
                copy(buffer, send, recv, chunk, target).start()

    above = lax.rem(me + 1, size)
    below = lax.rem(me + size - 1, size)

    @pl.loop(0, chunks + lag * last)
    def _(step):
        advance(step - lag * me, up, up_send, up_recv, me == 0, me == last, above, flags[0])
        advance(step - lag * (last - me), down, down_send, down_recv, me == last, me == 0, below, flags[1])

    @pl.loop(0, chunks)
    def _(chunk):
        @pl.when(me < last)
        def _():
            copy(up, up_send, up_recv, chunk, above).wait_send()

        @pl.when(me > 0)
        def _():
            copy(down, down_send, down_recv, chunk, below).wait_send()

        part = lax.select(flags[2] == 1, up[rows(chunk), :], own[rows(chunk), :])
        own[rows(chunk), :] = lax.select(flags[3] == 1, down[rows(chunk), :], part)

    store = pltpu.make_async_copy(own, out_hbm, local_sem)
    store.start()
    store.wait()


def chain(flags, payload, size):
    chunks = payload.shape[0] // chunk_rows
    return pl.pallas_call(
        functools.partial(chain_kernel, size, chunks),
        out_shape=jax.ShapeDtypeStruct(payload.shape, payload.dtype),
        in_specs=[pl.BlockSpec(memory_space=pltpu.SMEM), pl.BlockSpec(memory_space=pl.ANY)],
        out_specs=pl.BlockSpec(memory_space=pl.ANY),
        scratch_shapes=[pltpu.VMEM(payload.shape, payload.dtype) for _ in range(3)]
        + [pltpu.SemaphoreType.DMA((chunks,)) for _ in range(4)]
        + [pltpu.SemaphoreType.DMA],
        compiler_params=pltpu.CompilerParams(
            collective_id=0, has_side_effects=True, vmem_limit_bytes=48 * 2**20
        ),
    )(flags, payload)


def group_attention(queries, keys, values):
    sequence, head_count, head_size = queries.shape
    scores = jnp.einsum(
        "qhe,khe->hqk", queries, keys, preferred_element_type=jnp.float32
    ) * head_size ** (-0.5)
    position = lax.iota(jnp.int32, sequence)
    allowed = position[:, None] >= position[None, :]
    scores = jnp.where(allowed[None], scores, masked_value)
    maximum = jnp.max(scores, axis=-1, keepdims=True)
    weights = jnp.where(allowed[None], jnp.exp(scores - maximum), jnp.float32(0.0))
    totals = jnp.sum(weights, axis=-1)
    context = jnp.einsum(
        "hqk,khe->qhe", weights.astype(jnp.bfloat16), values, preferred_element_type=jnp.float32
    )
    context = context / jnp.transpose(totals)[:, :, None]
    return context.astype(jnp.bfloat16).reshape(sequence, head_count * head_size)


def body(
    attn_queries,
    attn_keys,
    attn_values,
    out_grad,
    out_proj,
    first_moment,
    second_moment,
    explore_noise,
    donor_index,
    copy_flag,
):
    group_count = lax.axis_size("fsdp")
    member_count = lax.axis_size("member")
    token_count, head_count, head_size = attn_queries.shape[1:]
    width = head_count * head_size
    row_count = out_proj.shape[1]
    group_heads = head_count // group_count
    stacked = jnp.stack(
        [
            a[0].reshape(token_count, group_count, group_heads * head_size)
            for a in (attn_queries, attn_keys, attn_values)
        ]
    )
    stacked = jnp.transpose(stacked, (2, 0, 1, 3))
    columns = jnp.transpose(out_grad[0].reshape(token_count, group_count, row_count), (1, 0, 2))
    stacked = lax.all_to_all(stacked, "fsdp", split_axis=0, concat_axis=0, tiled=True)
    columns = lax.all_to_all(columns, "fsdp", split_axis=0, concat_axis=0, tiled=True)
    columns = columns.reshape(group_count * token_count, row_count)
    heads = jnp.transpose(stacked, (1, 0, 2, 3)).reshape(
        3, group_count * token_count, group_heads, head_size
    )
    context = group_attention(heads[0], heads[1], heads[2])
    context = lax.all_gather(context, "fsdp", axis=0)
    context = jnp.transpose(context, (1, 0, 2)).reshape(group_count * token_count, width)
    gradient = lax.dot_general(
        columns, context, (((0,), (0,)), ((), ())), preferred_element_type=jnp.float32
    )
    moment_one = beta_first * first_moment[0] + (1.0 - beta_first) * gradient
    moment_two = beta_second * second_moment[0] + (1.0 - beta_second) * gradient * gradient
    bias_first = 1.0 - beta_first**100.0
    bias_second = 1.0 - beta_second**100.0
    step_size = moment_one / bias_first / (jnp.sqrt(moment_two / bias_second) + epsilon)
    weight_float = out_proj[0].astype(jnp.float32)
    updated = (weight_float - learn_rate * (step_size + decay_rate * weight_float)).astype(
        jnp.bfloat16
    )
    payload = jnp.concatenate(
        [updated, moment_one.astype(jnp.bfloat16), moment_two.astype(jnp.bfloat16)], axis=0
    )
    own_member = lax.axis_index("member")
    index = lax.iota(jnp.int32, member_count)
    goes_up = jnp.logical_and(copy_flag == 1, donor_index < index)
    goes_down = jnp.logical_and(copy_flag == 1, donor_index > index)
    until = index[:, None] >= index[None, :]
    up_rank = jnp.sum(jnp.logical_and(until, goes_up[None]).astype(jnp.int32), axis=1)
    down_rank = jnp.sum(jnp.logical_and(until, goes_down[None]).astype(jnp.int32), axis=1)
    rounds = jnp.maximum(jnp.max(up_rank), jnp.max(down_rank))

    def one_round(state):
        number, held = state
        up_now = jnp.logical_and(goes_up, up_rank == number + 1)
        down_now = jnp.logical_and(goes_down, down_rank == number + 1)
        mine = index == own_member
        from_me = donor_index == own_member
        flags = jnp.stack(
            [
                jnp.any(jnp.logical_and(up_now, from_me)),
                jnp.any(jnp.logical_and(down_now, from_me)),
                jnp.any(jnp.logical_and(up_now, mine)),
                jnp.any(jnp.logical_and(down_now, mine)),
            ]
        ).astype(jnp.int32)
        return number + 1, chain(flags, held, member_count)

    chosen = lax.while_loop(lambda state: state[0] < rounds, one_round, (jnp.int32(0), payload))[1]
    taken_weight = chosen[:row_count]
    flagged = jnp.any(jnp.logical_and(copy_flag == 1, index == own_member))
    perturbed = (taken_weight.astype(jnp.float32) + explore_noise[0].astype(jnp.float32)).astype(
        jnp.bfloat16
    )
    new_proj = jnp.where(flagged, perturbed, taken_weight)
    new_first = chosen[row_count : 2 * row_count].astype(jnp.float32)
    new_second = chosen[2 * row_count :].astype(jnp.float32)
    return (new_proj[None], new_first[None], new_second[None])


def solution(mesh):
    return jax.shard_map(
        body,
        mesh=mesh,
        in_specs=(
            P("member", "fsdp", None, None),
            P("member", "fsdp", None, None),
            P("member", "fsdp", None, None),
            P("member", "fsdp", None),
            P("member", "fsdp", None),
            P("member", "fsdp", None),
            P("member", "fsdp", None),
            P("member", "fsdp", None),
            P(),
            P(),
        ),
        out_specs=(P("member", "fsdp", None), P("member", "fsdp", None), P("member", "fsdp", None)),
        check_vma=False,
    )
```

```python
import functools

import jax
import jax.numpy as jnp
from jax import lax
from jax.experimental import pallas as pl
from jax.experimental.pallas import tpu as pltpu
from jax.sharding import PartitionSpec as P

masked_value = -1e30
beta_first = 0.9
beta_second = 0.95
learn_rate = 0.001
decay_rate = 0.1
epsilon = 1e-08
chunk_rows = 32
lag = 2
MESH = pl.DeviceIdType.MESH


def chain_kernel(size, chunks, flags, one_in, two_in, three_in, one_out, two_out, three_out, own, up, down, up_send, up_recv, down_send, down_recv, local_sem):
    me = lax.axis_index("member")
    last = size - 1
    length = one_in.shape[0]
    loads = [
        pltpu.make_async_copy(ref, own.at[pl.ds(place * length, length)], local_sem.at[place])
        for place, ref in enumerate((one_in, two_in, three_in))
    ]
    for load in loads:
        load.start()
    barrier = pltpu.get_barrier_semaphore()

    @pl.when(me > 0)
    def _():
        pl.semaphore_signal(barrier, inc=1, device_id={"member": me - 1}, device_id_type=MESH)

    @pl.when(me < last)
    def _():
        pl.semaphore_signal(barrier, inc=1, device_id={"member": me + 1}, device_id_type=MESH)

    @pl.when(jnp.logical_or(me == 0, me == last))
    def _():
        pl.semaphore_wait(barrier, 1)

    @pl.when(jnp.logical_and(me > 0, me < last))
    def _():
        pl.semaphore_wait(barrier, 2)

    for load in loads:
        load.wait()

    def rows(chunk):
        return pl.ds(pl.multiple_of(chunk * chunk_rows, chunk_rows), chunk_rows)

    def copy(buffer, send, recv, chunk, target):
        return pltpu.make_async_remote_copy(
            src_ref=buffer.at[rows(chunk)],
            dst_ref=buffer.at[rows(chunk)],
            send_sem=send.at[chunk],
            recv_sem=recv.at[chunk],
            device_id={"member": target},
            device_id_type=MESH,
        )

    def advance(chunk, buffer, send, recv, first, final, target, flag):
        @pl.when(jnp.logical_and(chunk >= 0, chunk < chunks))
        def _():
            @pl.when(first)
            def _():
                buffer[rows(chunk), :] = own[rows(chunk), :]

            @pl.when(jnp.logical_not(first))
            def _():
                copy(buffer, send, recv, chunk, target).wait_recv()
                buffer[rows(chunk), :] = lax.select(flag == 1, own[rows(chunk), :], buffer[rows(chunk), :])

            @pl.when(jnp.logical_not(final))
            def _():
                copy(buffer, send, recv, chunk, target).start()

    above = lax.rem(me + 1, size)
    below = lax.rem(me + size - 1, size)

    @pl.loop(0, chunks + lag * last)
    def _(step):
        advance(step - lag * me, up, up_send, up_recv, me == 0, me == last, above, flags[0])
        advance(step - lag * (last - me), down, down_send, down_recv, me == last, me == 0, below, flags[1])

    stores = [
        pltpu.make_async_copy(own.at[pl.ds(place * length, length)], ref, local_sem.at[place])
        for place, ref in enumerate((one_out, two_out, three_out))
    ]
    each = length // chunk_rows
    for place, store in enumerate(stores):

        @pl.loop(place * each, (place + 1) * each)
        def _(chunk):
            @pl.when(me < last)
            def _():
                copy(up, up_send, up_recv, chunk, above).wait_send()

            @pl.when(me > 0)
            def _():
                copy(down, down_send, down_recv, chunk, below).wait_send()

            part = lax.select(flags[2] == 1, up[rows(chunk), :], own[rows(chunk), :])
            own[rows(chunk), :] = lax.select(flags[3] == 1, down[rows(chunk), :], part)

        store.start()
    for store in stores:
        store.wait()


def chain(flags, payload, size):
    length, width = payload[0].shape
    kind = payload[0].dtype
    chunks = len(payload) * length // chunk_rows
    return pl.pallas_call(
        functools.partial(chain_kernel, size, chunks),
        out_shape=[jax.ShapeDtypeStruct((length, width), kind) for _ in payload],
        in_specs=[pl.BlockSpec(memory_space=pltpu.SMEM)]
        + [pl.BlockSpec(memory_space=pl.ANY) for _ in payload],
        out_specs=[pl.BlockSpec(memory_space=pl.ANY) for _ in payload],
        scratch_shapes=[pltpu.VMEM((len(payload) * length, width), kind) for _ in range(3)]
        + [pltpu.SemaphoreType.DMA((chunks,)) for _ in range(4)]
        + [pltpu.SemaphoreType.DMA((len(payload),))],
        input_output_aliases={place + 1: place for place in range(len(payload))},
        compiler_params=pltpu.CompilerParams(
            collective_id=0, has_side_effects=True, vmem_limit_bytes=48 * 2**20
        ),
    )(flags, *payload)


def step_kernel(grad_ref, context_ref, weight_ref, first_ref, second_ref, new_weight, new_first, new_second):
    gradient = jnp.dot(grad_ref[...], context_ref[...], preferred_element_type=jnp.float32)
    moment_one = beta_first * first_ref[...] + (1.0 - beta_first) * gradient
    moment_two = beta_second * second_ref[...] + (1.0 - beta_second) * gradient * gradient
    bias_first = 1.0 - beta_first**100.0
    bias_second = 1.0 - beta_second**100.0
    step_size = moment_one / bias_first / (jnp.sqrt(moment_two / bias_second) + epsilon)
    weight = weight_ref[...].astype(jnp.float32)
    updated = weight - learn_rate * (step_size + decay_rate * weight)
    new_weight[...] = updated.astype(new_weight.dtype)
    new_first[...] = moment_one.astype(new_first.dtype)
    new_second[...] = moment_two.astype(new_second.dtype)


def member_step(grad_columns, context, weight, first, second):
    rows, width = weight.shape
    tokens = context.shape[0]
    tile = 128
    wide = pl.BlockSpec((tile, width), lambda i: (i, 0))
    return pl.pallas_call(
        step_kernel,
        grid=(rows // tile,),
        out_shape=[jax.ShapeDtypeStruct((rows, width), jnp.bfloat16) for _ in range(3)],
        in_specs=[
            pl.BlockSpec((tile, tokens), lambda i: (i, 0)),
            pl.BlockSpec((tokens, width), lambda i: (0, 0)),
            wide,
            wide,
            wide,
        ],
        out_specs=[wide, wide, wide],
        compiler_params=pltpu.CompilerParams(vmem_limit_bytes=48 * 2**20),
    )(grad_columns, context, weight, first, second)


def group_attention(queries, keys, values):
    sequence, head_count, head_size = queries.shape
    scores = jnp.einsum(
        "qhe,khe->hqk", queries, keys, preferred_element_type=jnp.float32
    ) * head_size ** (-0.5)
    position = lax.iota(jnp.int32, sequence)
    allowed = position[:, None] >= position[None, :]
    scores = jnp.where(allowed[None], scores, masked_value)
    maximum = jnp.max(scores, axis=-1, keepdims=True)
    weights = jnp.where(allowed[None], jnp.exp(scores - maximum), jnp.float32(0.0))
    totals = jnp.sum(weights, axis=-1)
    context = jnp.einsum(
        "hqk,khe->qhe", weights.astype(jnp.bfloat16), values, preferred_element_type=jnp.float32
    )
    context = context / jnp.transpose(totals)[:, :, None]
    return context.astype(jnp.bfloat16).reshape(sequence, head_count * head_size)


def body(
    attn_queries,
    attn_keys,
    attn_values,
    out_grad,
    out_proj,
    first_moment,
    second_moment,
    explore_noise,
    donor_index,
    copy_flag,
):
    group_count = lax.axis_size("fsdp")
    member_count = lax.axis_size("member")
    token_count, head_count, head_size = attn_queries.shape[1:]
    width = head_count * head_size
    row_count = out_proj.shape[1]
    group_heads = head_count // group_count
    stacked = jnp.stack(
        [
            a[0].reshape(token_count, group_count, group_heads * head_size)
            for a in (attn_queries, attn_keys, attn_values)
        ]
    )
    stacked = jnp.transpose(stacked, (2, 0, 1, 3))
    columns = jnp.transpose(out_grad[0].reshape(token_count, group_count, row_count), (1, 0, 2))
    stacked = lax.all_to_all(stacked, "fsdp", split_axis=0, concat_axis=0, tiled=True)
    columns = lax.all_to_all(columns, "fsdp", split_axis=0, concat_axis=0, tiled=True)
    columns = columns.reshape(group_count * token_count, row_count)
    heads = jnp.transpose(stacked, (1, 0, 2, 3)).reshape(
        3, group_count * token_count, group_heads, head_size
    )
    context = group_attention(heads[0], heads[1], heads[2])
    context = lax.all_gather(context, "fsdp", axis=0)
    context = jnp.transpose(context, (1, 0, 2)).reshape(group_count * token_count, width)
    payload = tuple(
        member_step(columns.T, context, out_proj[0], first_moment[0], second_moment[0])
    )
    own_member = lax.axis_index("member")
    index = lax.iota(jnp.int32, member_count)
    goes_up = jnp.logical_and(copy_flag == 1, donor_index < index)
    goes_down = jnp.logical_and(copy_flag == 1, donor_index > index)
    until = index[:, None] >= index[None, :]
    up_rank = jnp.sum(jnp.logical_and(until, goes_up[None]).astype(jnp.int32), axis=1)
    down_rank = jnp.sum(jnp.logical_and(until, goes_down[None]).astype(jnp.int32), axis=1)
    rounds = jnp.maximum(jnp.max(up_rank), jnp.max(down_rank))

    def one_round(state):
        number, held = state
        up_now = jnp.logical_and(goes_up, up_rank == number + 1)
        down_now = jnp.logical_and(goes_down, down_rank == number + 1)
        mine = index == own_member
        from_me = donor_index == own_member
        flags = jnp.stack(
            [
                jnp.any(jnp.logical_and(up_now, from_me)),
                jnp.any(jnp.logical_and(down_now, from_me)),
                jnp.any(jnp.logical_and(up_now, mine)),
                jnp.any(jnp.logical_and(down_now, mine)),
            ]
        ).astype(jnp.int32)
        return number + 1, tuple(chain(flags, held, member_count))

    chosen = lax.while_loop(lambda state: state[0] < rounds, one_round, (jnp.int32(0), payload))[1]
    taken_weight, taken_first, taken_second = chosen
    flagged = jnp.any(jnp.logical_and(copy_flag == 1, index == own_member))
    perturbed = (taken_weight.astype(jnp.float32) + explore_noise[0].astype(jnp.float32)).astype(
        jnp.bfloat16
    )
    new_proj = jnp.where(flagged, perturbed, taken_weight)
    new_first = taken_first.astype(jnp.float32)
    new_second = taken_second.astype(jnp.float32)
    return (new_proj[None], new_first[None], new_second[None])


def solution(mesh):
    return jax.shard_map(
        body,
        mesh=mesh,
        in_specs=(
            P("member", "fsdp", None, None),
            P("member", "fsdp", None, None),
            P("member", "fsdp", None, None),
            P("member", "fsdp", None),
            P("member", "fsdp", None),
            P("member", "fsdp", None),
            P("member", "fsdp", None),
            P("member", "fsdp", None),
            P(),
            P(),
        ),
        out_specs=(P("member", "fsdp", None), P("member", "fsdp", None), P("member", "fsdp", None)),
        check_vma=False,
    )
```

```python
import functools

import jax
import jax.numpy as jnp
from jax import lax
from jax.experimental import pallas as pl
from jax.experimental.pallas import tpu as pltpu
from jax.sharding import PartitionSpec as P

masked_value = -1e30
beta_first = 0.9
beta_second = 0.95
learn_rate = 0.001
decay_rate = 0.1
epsilon = 1e-08
chunk_rows = 32
lag = 2
MESH = pl.DeviceIdType.MESH


def chain_kernel(size, chunks, flags, one_in, two_in, three_in, one_out, two_out, three_out, own, up, down, up_send, up_recv, down_send, down_recv, local_sem):
    me = lax.axis_index("member")
    last = size - 1
    length = one_in.shape[0]
    loads = [
        pltpu.make_async_copy(ref, own.at[pl.ds(place * length, length)], local_sem.at[place])
        for place, ref in enumerate((one_in, two_in, three_in))
    ]
    for load in loads:
        load.start()
    barrier = pltpu.get_barrier_semaphore()

    @pl.when(me > 0)
    def _():
        pl.semaphore_signal(barrier, inc=1, device_id={"member": me - 1}, device_id_type=MESH)

    @pl.when(me < last)
    def _():
        pl.semaphore_signal(barrier, inc=1, device_id={"member": me + 1}, device_id_type=MESH)

    @pl.when(jnp.logical_or(me == 0, me == last))
    def _():
        pl.semaphore_wait(barrier, 1)

    @pl.when(jnp.logical_and(me > 0, me < last))
    def _():
        pl.semaphore_wait(barrier, 2)

    for load in loads:
        load.wait()

    def rows(chunk):
        return pl.ds(pl.multiple_of(chunk * chunk_rows, chunk_rows), chunk_rows)

    def copy(buffer, send, recv, chunk, target):
        return pltpu.make_async_remote_copy(
            src_ref=buffer.at[rows(chunk)],
            dst_ref=buffer.at[rows(chunk)],
            send_sem=send.at[chunk],
            recv_sem=recv.at[chunk],
            device_id={"member": target},
            device_id_type=MESH,
        )

    def advance(chunk, buffer, send, recv, first, final, target, flag):
        @pl.when(jnp.logical_and(chunk >= 0, chunk < chunks))
        def _():
            @pl.when(first)
            def _():
                buffer[rows(chunk), :] = own[rows(chunk), :]

            @pl.when(jnp.logical_not(first))
            def _():
                copy(buffer, send, recv, chunk, target).wait_recv()
                buffer[rows(chunk), :] = lax.select(flag == 1, own[rows(chunk), :], buffer[rows(chunk), :])

            @pl.when(jnp.logical_not(final))
            def _():
                copy(buffer, send, recv, chunk, target).start()

    above = lax.rem(me + 1, size)
    below = lax.rem(me + size - 1, size)

    stores = [
        pltpu.make_async_copy(own.at[pl.ds(place * length, length)], ref, local_sem.at[place])
        for place, ref in enumerate((one_out, two_out, three_out))
    ]
    each = length // chunk_rows

    @pl.loop(0, chunks + lag * last)
    def _(step):
        advance(step - lag * me, up, up_send, up_recv, me == 0, me == last, above, flags[0])
        advance(step - lag * (last - me), down, down_send, down_recv, me == last, me == 0, below, flags[1])
        done = step - lag * last

        @pl.when(done >= 0)
        def _():
            part = lax.select(flags[2] == 1, up[rows(done), :], own[rows(done), :])
            own[rows(done), :] = lax.select(flags[3] == 1, down[rows(done), :], part)

        for place, store in enumerate(stores):
            pl.when(done == (place + 1) * each - 1)(store.start)

    @pl.loop(0, chunks)
    def _(chunk):
        @pl.when(me < last)
        def _():
            copy(up, up_send, up_recv, chunk, above).wait_send()

        @pl.when(me > 0)
        def _():
            copy(down, down_send, down_recv, chunk, below).wait_send()

    for store in stores:
        store.wait()


def chain(flags, payload, size):
    length, width = payload[0].shape
    kind = payload[0].dtype
    chunks = len(payload) * length // chunk_rows
    return pl.pallas_call(
        functools.partial(chain_kernel, size, chunks),
        out_shape=[jax.ShapeDtypeStruct((length, width), kind) for _ in payload],
        in_specs=[pl.BlockSpec(memory_space=pltpu.SMEM)]
        + [pl.BlockSpec(memory_space=pl.ANY) for _ in payload],
        out_specs=[pl.BlockSpec(memory_space=pl.ANY) for _ in payload],
        scratch_shapes=[pltpu.VMEM((len(payload) * length, width), kind) for _ in range(3)]
        + [pltpu.SemaphoreType.DMA((chunks,)) for _ in range(4)]
        + [pltpu.SemaphoreType.DMA((len(payload),))],
        input_output_aliases={place + 1: place for place in range(len(payload))},
        compiler_params=pltpu.CompilerParams(
            collective_id=0, has_side_effects=True, vmem_limit_bytes=48 * 2**20
        ),
    )(flags, *payload)


def step_kernel(grad_ref, context_ref, weight_ref, first_ref, second_ref, new_weight, new_first, new_second):
    gradient = jnp.dot(grad_ref[...], context_ref[...], preferred_element_type=jnp.float32)
    moment_one = beta_first * first_ref[...] + (1.0 - beta_first) * gradient
    moment_two = beta_second * second_ref[...] + (1.0 - beta_second) * gradient * gradient
    bias_first = 1.0 - beta_first**100.0
    bias_second = 1.0 - beta_second**100.0
    step_size = moment_one / bias_first / (jnp.sqrt(moment_two / bias_second) + epsilon)
    weight = weight_ref[...].astype(jnp.float32)
    updated = weight - learn_rate * (step_size + decay_rate * weight)
    new_weight[...] = updated.astype(new_weight.dtype)
    new_first[...] = moment_one.astype(new_first.dtype)
    new_second[...] = moment_two.astype(new_second.dtype)


def member_step(grad_columns, context, weight, first, second):
    rows, width = weight.shape
    tokens = context.shape[0]
    tile = 128
    wide = pl.BlockSpec((tile, width), lambda i: (i, 0))
    return pl.pallas_call(
        step_kernel,
        grid=(rows // tile,),
        out_shape=[jax.ShapeDtypeStruct((rows, width), jnp.bfloat16) for _ in range(3)],
        in_specs=[
            pl.BlockSpec((tile, tokens), lambda i: (i, 0)),
            pl.BlockSpec((tokens, width), lambda i: (0, 0)),
            wide,
            wide,
            wide,
        ],
        out_specs=[wide, wide, wide],
        compiler_params=pltpu.CompilerParams(vmem_limit_bytes=48 * 2**20),
    )(grad_columns, context, weight, first, second)


def group_attention(queries, keys, values):
    sequence, head_count, head_size = queries.shape
    scores = jnp.einsum(
        "qhe,khe->hqk", queries, keys, preferred_element_type=jnp.float32
    ) * head_size ** (-0.5)
    position = lax.iota(jnp.int32, sequence)
    allowed = position[:, None] >= position[None, :]
    scores = jnp.where(allowed[None], scores, masked_value)
    maximum = jnp.max(scores, axis=-1, keepdims=True)
    weights = jnp.where(allowed[None], jnp.exp(scores - maximum), jnp.float32(0.0))
    totals = jnp.sum(weights, axis=-1)
    context = jnp.einsum(
        "hqk,khe->qhe", weights.astype(jnp.bfloat16), values, preferred_element_type=jnp.float32
    )
    context = context / jnp.transpose(totals)[:, :, None]
    return context.astype(jnp.bfloat16).reshape(sequence, head_count * head_size)


def body(
    attn_queries,
    attn_keys,
    attn_values,
    out_grad,
    out_proj,
    first_moment,
    second_moment,
    explore_noise,
    donor_index,
    copy_flag,
):
    group_count = lax.axis_size("fsdp")
    member_count = lax.axis_size("member")
    token_count, head_count, head_size = attn_queries.shape[1:]
    width = head_count * head_size
    row_count = out_proj.shape[1]
    group_heads = head_count // group_count
    stacked = jnp.stack(
        [
            a[0].reshape(token_count, group_count, group_heads * head_size)
            for a in (attn_queries, attn_keys, attn_values)
        ]
    )
    stacked = jnp.transpose(stacked, (2, 0, 1, 3))
    columns = jnp.transpose(out_grad[0].reshape(token_count, group_count, row_count), (1, 0, 2))
    stacked = lax.all_to_all(stacked, "fsdp", split_axis=0, concat_axis=0, tiled=True)
    columns = lax.all_to_all(columns, "fsdp", split_axis=0, concat_axis=0, tiled=True)
    columns = columns.reshape(group_count * token_count, row_count)
    heads = jnp.transpose(stacked, (1, 0, 2, 3)).reshape(
        3, group_count * token_count, group_heads, head_size
    )
    context = group_attention(heads[0], heads[1], heads[2])
    context = lax.all_gather(context, "fsdp", axis=0)
    context = jnp.transpose(context, (1, 0, 2)).reshape(group_count * token_count, width)
    payload = tuple(
        member_step(columns.T, context, out_proj[0], first_moment[0], second_moment[0])
    )
    own_member = lax.axis_index("member")
    index = lax.iota(jnp.int32, member_count)
    goes_up = jnp.logical_and(copy_flag == 1, donor_index < index)
    goes_down = jnp.logical_and(copy_flag == 1, donor_index > index)
    until = index[:, None] >= index[None, :]
    up_rank = jnp.sum(jnp.logical_and(until, goes_up[None]).astype(jnp.int32), axis=1)
    down_rank = jnp.sum(jnp.logical_and(until, goes_down[None]).astype(jnp.int32), axis=1)
    rounds = jnp.maximum(jnp.max(up_rank), jnp.max(down_rank))

    def one_round(state):
        number, held = state
        up_now = jnp.logical_and(goes_up, up_rank == number + 1)
        down_now = jnp.logical_and(goes_down, down_rank == number + 1)
        mine = index == own_member
        from_me = donor_index == own_member
        flags = jnp.stack(
            [
                jnp.any(jnp.logical_and(up_now, from_me)),
                jnp.any(jnp.logical_and(down_now, from_me)),
                jnp.any(jnp.logical_and(up_now, mine)),
                jnp.any(jnp.logical_and(down_now, mine)),
            ]
        ).astype(jnp.int32)
        return number + 1, tuple(chain(flags, held, member_count))

    chosen = lax.while_loop(lambda state: state[0] < rounds, one_round, (jnp.int32(0), payload))[1]
    taken_weight, taken_first, taken_second = chosen
    flagged = jnp.any(jnp.logical_and(copy_flag == 1, index == own_member))
    perturbed = (taken_weight.astype(jnp.float32) + explore_noise[0].astype(jnp.float32)).astype(
        jnp.bfloat16
    )
    new_proj = jnp.where(flagged, perturbed, taken_weight)
    new_first = taken_first.astype(jnp.float32)
    new_second = taken_second.astype(jnp.float32)
    return (new_proj[None], new_first[None], new_second[None])


def solution(mesh):
    return jax.shard_map(
        body,
        mesh=mesh,
        in_specs=(
            P("member", "fsdp", None, None),
            P("member", "fsdp", None, None),
            P("member", "fsdp", None, None),
            P("member", "fsdp", None),
            P("member", "fsdp", None),
            P("member", "fsdp", None),
            P("member", "fsdp", None),
            P("member", "fsdp", None),
            P(),
            P(),
        ),
        out_specs=(P("member", "fsdp", None), P("member", "fsdp", None), P("member", "fsdp", None)),
        check_vma=False,
    )
```
